256 devices in a mesh: ep: 32 (over z, x_lo, core), dp: 8 (over y, x_hi).
Axes of the slice: x: 4 (x_hi: 2, x_lo: 2; x = x_hi * 2 + x_lo), y: 4, z: 8, core: 2. Of those that a mesh axis runs over, the one named last changes fastest.
Arguments:
- grad_out: bfloat16 [49152, 3584], P(('ep', 'dp')), may hold values from -0.59765625 to 0.59765625
- route_probs: float32 [49152, 8], P(('ep', 'dp')), may hold values from 0.02 to 0.6
- routes: int32 [49152, 8], P(('ep', 'dp')), may hold values from 0 to 127, as said below
- hidden_saved: bfloat16 [256, 768, 2048], P(('ep', 'dp')), may hold values from -6 to 6
Outputs:
- grad_down: bfloat16 [2048, 114688], P('dp', 'ep')
The draws below stay inside these ranges and needn't reach their ends.
Inputs may be any that keep to these rules, and one draw needn't show every extreme that they name: `routes`: each row names 8 different experts. In each aligned block of 192 rows (the rows of one device) no expert is named by more than 24 rows, and one expert whose index modulo 4 is below 1 is named by exactly 24 rows in every block.
All inputs are finite; a program needn't handle non-finite values.
Results may differ from the reference program's by a relative error of at most 0.015.
Values may be sent and summed in bfloat16 or wider, within the bound.
No kernel may reach another device: no remote copies, remote signals or barrier semaphores. Data moves between devices by JAX's collectives and lax.ppermute only.
A program may use at most 64 MiB of HBM per device.

```python
import math
import jax
import jax.numpy as jnp
from jax import lax

D = 3584
FF = 2048
TOP = 8
EXP_DEV = 4
FLIGHT = 1
TOK_DEV = 192
EXPERTS = 128
MOST = 24
TOKENS = 49152
N_EP = 32
N_DP = 8


def block_routes(block_key, hot_expert):
    route_total = TOK_DEV * TOP
    others_count = EXPERTS - 1
    base_load = (route_total - MOST) // others_count
    extra_load = route_total - MOST - base_load * others_count
    spread_max = max(min(base_load, MOST - base_load - 1), 0)
    order_key, spread_key, token_key, column_key = jax.random.split(block_key, 4)
    shuffled = jax.random.permutation(order_key, others_count).astype(jnp.int32)
    other_ids = shuffled + (shuffled >= hot_expert).astype(jnp.int32)
    loads = base_load + (jnp.arange(others_count, dtype=jnp.int32) < extra_load).astype(jnp.int32)
    spread = jax.random.randint(spread_key, (others_count // 2,), 0, spread_max + 1).astype(jnp.int32)
    signed = jnp.stack([spread, -spread], axis=1).reshape(-1)
    signed = jnp.concatenate([signed, jnp.zeros((others_count % 2,), jnp.int32)])
    loads = loads + signed
    all_ids = jnp.concatenate([hot_expert.reshape(1).astype(jnp.int32), other_ids])
    all_loads = jnp.concatenate([jnp.full((1,), MOST, jnp.int32), loads])
    run_ends = jnp.cumsum(all_loads).astype(jnp.int32)
    places = jnp.arange(route_total, dtype=jnp.int32)
    which = jnp.searchsorted(run_ends, places, side='right')
    experts_flat = all_ids[which]
    grid = experts_flat.reshape(TOP, TOK_DEV).T
    grid = grid[jax.random.permutation(token_key, TOK_DEV)]
    scores = jax.random.randint(column_key, (TOK_DEV, TOP), 0, 1024) * TOP + jnp.arange(TOP, dtype=jnp.int32)
    ordering = jnp.argsort(scores, axis=1, stable=True)
    return jnp.take_along_axis(grid, ordering, axis=1).astype(jnp.int32)


def draw_routes(key, part):
    key = jax.random.fold_in(key, 7)
    member_key, rank_key, block_key = jax.random.split(key, 3)
    expert_ranks = EXPERTS // EXP_DEV
    hot_expert = jax.random.randint(rank_key, (), 0, expert_ranks) * EXP_DEV + jax.random.randint(member_key, (), 0, FLIGHT)
    block_keys = jax.random.split(block_key, TOKENS // TOK_DEV)
    routed = jax.vmap(lambda one_key: block_routes(one_key, hot_expert))(block_keys)
    return routed.reshape(TOKENS, TOP)


def level_of(rng, shape, cuts, least, largest):
    loudness = 1.0
    for dim, blocks in cuts:
        steps = jax.random.uniform(jax.random.fold_in(jax.random.fold_in(rng, 6), dim), (blocks,), jnp.float32, least / len(cuts), largest / len(cuts))
        loudness = loudness * jnp.repeat(jnp.exp(steps), shape[dim] // blocks).reshape((-1,) + (1,) * (len(shape) - 1 - dim))
    return loudness


def gaussian(rng, shape, scale, bound, cuts=(), kind=jnp.bfloat16):
    result = jax.random.normal(rng, shape, jnp.float32) * scale
    if len(cuts) > 0:
        result = level_of(rng, shape, cuts, -0.22, 0.18) * result
    return jnp.clip(result, min=-bound, max=bound).astype(kind)


def setup_inputs(seed: int = 0) -> dict:
    arg_keys = jax.random.split(jax.random.key(seed), 5)
    return {
        "grad_out": gaussian(arg_keys[0], (TOKENS, D), 0.1, 0.59765625, ((0, 256),)),
        "route_probs": jnp.clip(jnp.exp(math.log(0.6) - 3.4011974 * jax.random.uniform(arg_keys[1], (TOKENS, TOP), jnp.float32) ** level_of(arg_keys[1], (TOKENS, TOP), ((0, 256),), -0.2, 0.2)), 0.02, 0.6),
        "routes": draw_routes(jax.random.fold_in(arg_keys[4], 71), 0),
        "hidden_saved": gaussian(arg_keys[3], (N_EP * N_DP * FLIGHT, N_EP * MOST, FF), 1.0, 6.0, ((0, 256),)),
    }


def reference(grad_out, route_probs, routes, hidden_saved):
    slot_count = N_EP * MOST
    columns = N_EP * FLIGHT
    route_grid = routes.reshape(N_EP, N_DP, TOK_DEV, TOP).astype(jnp.int32)
    prob_grid = route_probs.reshape(N_EP, N_DP, TOK_DEV, TOP)
    expert_ids = jnp.arange(EXPERTS, dtype=jnp.int32)
    naming = jnp.sum((route_grid[..., None] == expert_ids).astype(jnp.int32), axis=3)
    earlier = jnp.cumsum(naming, axis=2) - naming
    position = jnp.take_along_axis(earlier, route_grid, axis=3).astype(jnp.int32)
    owner_rank = route_grid // EXP_DEV
    local_index = route_grid % EXP_DEV
    in_flight = local_index < FLIGHT
    source_rank = jnp.arange(N_EP, dtype=jnp.int32)[:, None, None, None]
    dp_index = jnp.arange(N_DP, dtype=jnp.int32)[None, :, None, None]
    token_index = jnp.arange(TOK_DEV, dtype=jnp.int32)[None, None, :, None]
    column = owner_rank * FLIGHT + local_index
    flat_size = columns * N_DP * slot_count
    target = (column * N_DP + dp_index) * slot_count + source_rank * MOST + position
    target = jnp.where(in_flight, target, flat_size).astype(jnp.int32).reshape(-1)
    global_row = (source_rank * N_DP + dp_index) * TOK_DEV + token_index
    global_row = jnp.broadcast_to(global_row, route_grid.shape).astype(jnp.int32).reshape(-1)
    source_row = jnp.zeros((flat_size,), jnp.int32).at[target].set(global_row, mode="drop")
    source_row = source_row.reshape(columns, N_DP, slot_count)
    weight = jnp.zeros((flat_size,), jnp.float32).at[target].set(prob_grid.reshape(-1), mode="drop")
    weight = weight.reshape(columns, N_DP, slot_count)
    saved = hidden_saved.reshape(N_EP, N_DP, FLIGHT, slot_count, FF)

    def expert_gradient(column_index):
        rank_index = column_index // FLIGHT
        member = column_index % FLIGHT
        rows_here = source_row[column_index]
        scaled = (weight[column_index][..., None] * grad_out[rows_here].astype(jnp.float32)).astype(jnp.bfloat16)
        hidden_rows = saved[rank_index, :, member]
        partial_sums = jnp.einsum("jsk,jsd->jkd", hidden_rows.astype(jnp.float32), scaled.astype(jnp.float32))
        rounded = lax.optimization_barrier(partial_sums.astype(jnp.bfloat16)).astype(jnp.float32)
        return jnp.sum(rounded, axis=0).astype(jnp.bfloat16)

    per_expert = lax.map(expert_gradient, jnp.arange(columns, dtype=jnp.int32))
    return jnp.transpose(per_expert, (1, 0, 2)).reshape(FF, columns * D)
```

```python
import functools

import jax
import jax.numpy as jnp
from jax import lax
from jax.experimental import pallas as pl
from jax.experimental.pallas import tpu as pltpu
from jax.sharding import PartitionSpec as P

EXP_DEV = 4
CHUNKS = 4


def rows_kernel(columns, capacity, chunks, routes_ref, probs_ref, grad_ref, *out_refs):
    top, tok = routes_ref.shape
    ids = lax.broadcasted_iota(jnp.int32, (columns, tok), 0) * EXP_DEV
    named = jnp.zeros((columns, tok), jnp.float32)
    prob = jnp.zeros((columns, tok), jnp.float32)
    for k in range(top):
        hit = routes_ref[k : k + 1, :] == ids
        named = named + jnp.where(hit, 1.0, 0.0)
        prob = prob + jnp.where(hit, probs_ref[k : k + 1, :], 0.0)
    row = lax.broadcasted_iota(jnp.int32, (tok, tok), 0)
    col = lax.broadcasted_iota(jnp.int32, (tok, tok), 1)
    earlier = jnp.where(row < col, 1.0, 0.0).astype(jnp.bfloat16)
    slot = jnp.dot(named.astype(jnp.bfloat16), earlier, preferred_element_type=jnp.float32)
    slot = jnp.where(named > 0.0, slot, -1.0).astype(jnp.int32)
    places = lax.broadcasted_iota(jnp.int32, (columns, capacity, tok), 1)
    pick = slot[:, None, :] == places
    weight = jnp.sum(jnp.where(pick, prob[:, None, :], 0.0), axis=2, keepdims=True)
    weight = weight.reshape(columns * capacity, 1)
    pick = jnp.where(pick, 1.0, 0.0).reshape(columns * capacity, tok).astype(jnp.bfloat16)
    width = grad_ref.shape[1] // chunks
    for c in range(chunks):
        taken = jnp.dot(
            pick, grad_ref[:, c * width : (c + 1) * width], preferred_element_type=jnp.float32
        )
        out_refs[c][...] = (weight * taken).astype(jnp.bfloat16)


def expert_term(hidden_rows, arrived):
    return lax.dot_general(
        hidden_rows, arrived, (((0,), (0,)), ((), ())), preferred_element_type=jnp.float32
    ).astype(jnp.bfloat16)


def shards(grad_out, route_probs, routes, hidden_saved):
    tok, model_cols = grad_out.shape
    flight, slot_count, hidden = hidden_saved.shape
    ranks = lax.axis_size("ep")
    capacity = slot_count // ranks
    width = model_cols // CHUNKS
    outgoing = pl.pallas_call(
        functools.partial(rows_kernel, ranks, capacity, CHUNKS),
        out_shape=[jax.ShapeDtypeStruct((slot_count, width), jnp.bfloat16)] * CHUNKS,
        compiler_params=pltpu.CompilerParams(vmem_limit_bytes=48 * 1024 * 1024),
    )(routes.T, route_probs.T, grad_out)
    parts = []
    for c in range(CHUNKS):
        rows = outgoing[c].reshape(ranks, capacity, width)
        arrived = lax.all_to_all(rows, "ep", split_axis=0, concat_axis=0, tiled=True)
        term = expert_term(hidden_saved[0], arrived.reshape(slot_count, width))
        parts.append(lax.psum_scatter(term, "dp", scatter_dimension=0, tiled=True))
    return jnp.concatenate(parts, axis=1)


def solution(mesh):
    in_specs = (
        P(("ep", "dp"), None),
        P(("ep", "dp"), None),
        P(("ep", "dp"), None),
        P(("ep", "dp"), None, None),
    )
    return jax.shard_map(
        shards, mesh=mesh, in_specs=in_specs, out_specs=P("dp", "ep"), check_vma=False
    )
```

```python
import functools

import jax
import jax.numpy as jnp
from jax import lax
from jax.experimental import pallas as pl
from jax.experimental.pallas import tpu as pltpu
from jax.sharding import PartitionSpec as P

EXP_DEV = 4
WIDTHS = (768, 1280, 1024, 512)
VMEM = 56 * 1024 * 1024
SPARE = 10 * 1024 * 1024


def rows_kernel(columns, capacity, widths, routes_ref, probs_ref, grad_ref, *out_refs):
    top, tok = routes_ref.shape
    ids = lax.broadcasted_iota(jnp.int32, (columns, tok), 0) * EXP_DEV
    named = jnp.zeros((columns, tok), jnp.float32)
    prob = jnp.zeros((columns, tok), jnp.float32)
    for k in range(top):
        hit = routes_ref[k : k + 1, :] == ids
        named = named + jnp.where(hit, 1.0, 0.0)
        prob = prob + jnp.where(hit, probs_ref[k : k + 1, :], 0.0)
    row = lax.broadcasted_iota(jnp.int32, (tok, tok), 0)
    col = lax.broadcasted_iota(jnp.int32, (tok, tok), 1)
    earlier = jnp.where(row < col, 1.0, 0.0).astype(jnp.bfloat16)
    slot = jnp.dot(named.astype(jnp.bfloat16), earlier, preferred_element_type=jnp.float32)
    slot = jnp.where(named > 0.0, slot, -1.0).astype(jnp.int32)
    places = lax.broadcasted_iota(jnp.int32, (columns, capacity, tok), 1)
    pick = slot[:, None, :] == places
    weight = jnp.sum(jnp.where(pick, prob[:, None, :], 0.0), axis=2, keepdims=True)
    weight = weight.reshape(columns * capacity, 1)
    pick = jnp.where(pick, 1.0, 0.0).reshape(columns * capacity, tok).astype(jnp.bfloat16)
    start = 0
    for c, width in enumerate(widths):
        taken = jnp.dot(
            pick, grad_ref[:, start : start + width], preferred_element_type=jnp.float32
        )
        out_refs[c][...] = (weight * taken).astype(jnp.bfloat16)
        start += width


def product(hidden_ref, at, size, rows):
    return lax.dot_general(
        hidden_ref[:, pl.ds(pl.multiple_of(at, size), size)],
        rows,
        (((0,), (0,)), ((), ())),
        preferred_element_type=jnp.float32,
    )


def first_terms(place, hidden_ref, ins, outs):
    (arrived_ref,) = ins
    size = hidden_ref.shape[1] // 4
    half = arrived_ref.shape[1] // 2
    y = place[0]
    one, two = y ^ 1, 3 - y
    for h, near in enumerate((one, two)):
        rows = arrived_ref[:, h * half : (h + 1) * half]
        for i, block in enumerate((two ^ 1, near)):
            outs[h][i * size : (i + 1) * size, :] = product(
                hidden_ref, block * size, size, rows
            ).astype(jnp.bfloat16)


def second_terms(place, hidden_ref, ins, outs):
    arrived_ref, *got = ins
    size = hidden_ref.shape[1] // 4
    half = arrived_ref.shape[1] // 2
    y = place[0]
    for h, far in enumerate((3 - y, y ^ 1)):
        rows = arrived_ref[:, h * half : (h + 1) * half]
        mine = product(hidden_ref, far * size, size, rows)
        outs[h][...] = (mine + got[h][:size, :].astype(jnp.float32)).astype(jnp.bfloat16)


def third_terms(place, hidden_ref, ins, outs):
    arrived_ref, *rest = ins
    got, more = rest[:2], rest[2:]
    size = hidden_ref.shape[1] // 4
    part = size // 2
    half = arrived_ref.shape[1] // 2
    y, xh = place[0], place[1]
    for out_ref, x in zip(outs, (1 - xh, xh)):
        at = pl.multiple_of(x * part, part)
        for h in range(2):
            cols = slice(h * half, (h + 1) * half)
            total = product(hidden_ref, y * size + x * part, part, arrived_ref[:, cols])
            total = total + got[h][pl.ds(size + at, part), :].astype(jnp.float32)
            total = total + more[h][pl.ds(at, part), :].astype(jnp.float32)
            out_ref[:, cols] = total.astype(out_ref.dtype)


def last_sum(place, hidden_ref, ins, outs):
    keep_ref, last_ref = ins
    outs[0][...] = (keep_ref[...] + last_ref[...].astype(jnp.float32)).astype(jnp.bfloat16)


def tick_kernel(jobs, passed, place_ref, hidden_ref, *refs):
    ins = refs[: sum(n for _, n, _ in jobs)]
    outs = refs[len(ins) + passed :]
    i = o = 0
    for job, n_in, n_out in jobs:
        job(place_ref, hidden_ref, ins[i : i + n_in], outs[o : o + n_out])
        i, o = i + n_in, o + n_out


def tick(place, hidden, jobs, passed):
    ins = [x for _, given, _ in jobs for x in given]
    shapes = [s for _, _, made in jobs for s in made]
    counts = [(job, len(given), len(made)) for job, given, made in jobs]
    vmem, anywhere = pl.BlockSpec(memory_space=pltpu.VMEM), pl.BlockSpec(memory_space=pl.ANY)
    held = sum(x.size * x.dtype.itemsize for x in [hidden, *ins, *shapes])
    res = pl.pallas_call(
        functools.partial(tick_kernel, counts, len(passed)),
        in_specs=[pl.BlockSpec(memory_space=pltpu.SMEM), vmem]
        + [vmem] * len(ins)
        + [anywhere] * len(passed),
        out_specs=[vmem] * len(shapes) + [anywhere] * len(passed),
        out_shape=shapes + [jax.ShapeDtypeStruct(p.shape, p.dtype) for p in passed],
        input_output_aliases={2 + len(ins) + i: len(shapes) + i for i in range(len(passed))},
        compiler_params=pltpu.CompilerParams(vmem_limit_bytes=min(VMEM, held + SPARE)),
    )(place, hidden, *ins, *passed)
    made, at = [], 0
    for _, _, n_out in counts:
        made.append(res[at : at + n_out])
        at += n_out
    return made, res[at:]


def shards(grad_out, route_probs, routes, hidden_saved):
    tok, model_cols = grad_out.shape
    flight, slot_count, hidden = hidden_saved.shape
    ranks = lax.axis_size("ep")
    peers = lax.axis_size("dp")
    capacity = slot_count // ranks
    dp = lax.axis_index("dp")
    place = jnp.stack([dp // 2, dp % 2]).astype(jnp.int32)
    outgoing = pl.pallas_call(
        functools.partial(rows_kernel, ranks, capacity, WIDTHS),
        out_shape=[jax.ShapeDtypeStruct((slot_count, w), jnp.bfloat16) for w in WIDTHS],
        compiler_params=pltpu.CompilerParams(vmem_limit_bytes=VMEM),
    )(routes.T, route_probs.T, grad_out)

    to_a = [(i, i ^ 2) for i in range(peers)]
    to_b = [(i, (3 - i // 2) * 2 + i % 2) for i in range(peers)]
    to_x = [(i, i ^ 1) for i in range(peers)]
    hid = hidden_saved[0]
    count = len(WIDTHS)

    def shape(rows, cols, dtype=jnp.bfloat16):
        return jax.ShapeDtypeStruct((rows, cols), dtype)

    arrived, got, more, keep, last, out = {}, {}, {}, {}, {}, {}
    rows = outgoing[0]
    for t in range(count + 4):
        if t > 0:
            jobs, chunks = [], []
            for back, body in ((1, first_terms), (2, second_terms), (3, third_terms), (4, last_sum)):
                c = t - back
                if not 0 <= c < count:
                    continue
                w = WIDTHS[c]
                if back == 1:
                    job = (body, [arrived[c]], [shape(hidden // 2, w // 2)] * 2)
                elif back == 2:
                    job = (body, [arrived[c], *got[c]], [shape(hidden // 4, w // 2)] * 2)
                elif back == 3:
                    job = (
                        body,
                        [arrived[c], *got[c], *more[c]],
                        [shape(hidden // peers, w), shape(hidden // peers, w, jnp.float32)],
                    )
                else:
                    job = (body, [keep[c], last[c]], [shape(hidden // peers, w)])
                jobs.append(job)
                chunks.append((back, c))
            passed = [outgoing[t]] if t < count else []
            made, passed = tick(place, hid, jobs, passed)
            for (back, c), made_here in zip(chunks, made):
                if back == 1:
                    got[c] = [lax.ppermute(s, "dp", to) for s, to in zip(made_here, (to_a, to_b))]
                elif back == 2:
                    more[c] = [lax.ppermute(s, "dp", to) for s, to in zip(made_here, (to_b, to_a))]
                elif back == 3:
                    last[c], keep[c] = lax.ppermute(made_here[0], "dp", to_x), made_here[1]
                else:
                    out[c] = made_here[0]
            if t < count:
                rows = passed[0]
        if t < count:
            came = lax.all_to_all(
                rows.reshape(ranks, capacity, WIDTHS[t]), "ep", split_axis=0, concat_axis=0, tiled=True
            )
            arrived[t] = came.reshape(slot_count, WIDTHS[t])
    return jnp.concatenate([out[c] for c in range(count)], axis=1)


def solution(mesh):
    in_specs = (
        P(("ep", "dp"), None),
        P(("ep", "dp"), None),
        P(("ep", "dp"), None),
        P(("ep", "dp"), None, None),
    )
    return jax.shard_map(
        shards, mesh=mesh, in_specs=in_specs, out_specs=P("dp", "ep"), check_vma=False
    )
```

```python
import functools

import jax
import jax.numpy as jnp
from jax import lax
from jax.experimental import pallas as pl
from jax.experimental.pallas import tpu as pltpu
from jax.sharding import PartitionSpec as P

EXP_DEV = 4
TWO = ((0, 1, 2), (1, 0, 2))
THREE = ((0, 1, 2), (1, 2, 0), (2, 0, 1))
WIDTHS = ((512, 512), (768, 768), (384, 384, 256))
ORDERS = (TWO, TWO, THREE)
VMEM = 16 * 1024 * 1024
STEPS = (
    ((0, 0),),
    ((0, 1),),
    ((1, 0),),
    ((2, 0),),
    ((3, 0),),
    ((0, 2),),
    ((1, 1),),
    ((2, 1), (4, 0)),
    ((1, 2),),
    ((3, 1),),
    ((2, 2), (4, 1)),
    ((3, 2),),
    ((4, 2),),
)


def rows_kernel(columns, capacity, start, routes_ref, probs_ref, grad_ref, token_ref, out_ref, _):
    top, tok = routes_ref.shape
    ids = lax.broadcasted_iota(jnp.int32, (columns, tok), 0) * EXP_DEV
    named = jnp.zeros((columns, tok), jnp.float32)
    prob = jnp.zeros((columns, tok), jnp.float32)
    for k in range(top):
        hit = routes_ref[k : k + 1, :] == ids
        named = named + jnp.where(hit, 1.0, 0.0)
        prob = prob + jnp.where(hit, probs_ref[k : k + 1, :], 0.0)
    row = lax.broadcasted_iota(jnp.int32, (tok, tok), 0)
    col = lax.broadcasted_iota(jnp.int32, (tok, tok), 1)
    earlier = jnp.where(row < col, 1.0, 0.0).astype(jnp.bfloat16)
    slot = jnp.dot(named.astype(jnp.bfloat16), earlier, preferred_element_type=jnp.float32)
    slot = jnp.where(named > 0.0, slot, -1.0).astype(jnp.int32)
    places = lax.broadcasted_iota(jnp.int32, (columns, capacity, tok), 1)
    pick = slot[:, None, :] == places
    weight = jnp.sum(jnp.where(pick, prob[:, None, :], 0.0), axis=2, keepdims=True)
    weight = weight.reshape(columns * capacity, 1)
    pick = jnp.where(pick, 1.0, 0.0).reshape(columns * capacity, tok).astype(jnp.bfloat16)
    width = out_ref.shape[1]
    taken = jnp.dot(pick, grad_ref[:, start : start + width], preferred_element_type=jnp.float32)
    out_ref[...] = (weight * taken).astype(jnp.bfloat16)


def block_of(place_ref, order, bits):
    y, xh = place_ref[0], place_ref[1]
    for kind, bit in zip(order, bits):
        if bit:
            y, xh = (y ^ 1, xh) if kind == 0 else (3 - y, xh) if kind == 1 else (y, 1 - xh)
    return y * 2 + xh


def product(place_ref, hidden_ref, size, order, bits, rows):
    at = pl.multiple_of(block_of(place_ref, order, bits) * size, size)
    return lax.dot_general(
        hidden_ref[:, pl.ds(at, size)],
        rows,
        (((0,), (0,)), ((), ())),
        preferred_element_type=jnp.float32,
    )


def terms(kind, orders, size, place_ref, hidden_ref, ins, outs):
    arrived_ref, came = ins[0], ins[1:]
    start = 0
    for part, order in enumerate(orders):
        width = outs[part].shape[1]
        rows = arrived_ref[:, start : start + width]
        start += width
        earlier = [came[e * len(orders) + part] for e in range(kind - 1)]
        if kind == 1:
            targets = [(outs[part], (1, i, j)) for i in (1, 0) for j in (1, 0)]
        elif kind == 2:
            targets = [(outs[part], (0, 1, j)) for j in (1, 0)]
        else:
            targets = [(outs[part], (0, 0, 1)), (outs[len(orders) + part], (0, 0, 0))]
        filled = {}
        for out_ref, bits in targets:
            total = product(place_ref, hidden_ref, size, order, bits, rows)
            if kind > 1:
                at = (2 * (1 - bits[1]) + 1 - bits[2]) * size
                total = total + earlier[0][at : at + size, :].astype(jnp.float32)
            if kind > 2:
                at = (1 - bits[2]) * size
                total = total + earlier[1][at : at + size, :].astype(jnp.float32)
            at = filled.get(id(out_ref), 0)
            out_ref[at : at + size, :] = total.astype(out_ref.dtype)
            filled[id(out_ref)] = at + size


def last_sum(ins, outs):
    start = 0
    parts = len(ins) // 2
    for part in range(parts):
        width = ins[part].shape[1]
        total = ins[part][...] + ins[parts + part][...].astype(jnp.float32)
        outs[0][:, start : start + width] = total.astype(jnp.bfloat16)
        start += width


def step_kernel(size, jobs, place_ref, hidden_ref, *refs):
    ins = refs[: sum(n for _, _, n, _ in jobs)]
    outs = refs[len(ins) + 1 :]
    i = o = 0
    for kind, orders, n_in, n_out in jobs:
        if kind == 4:
            last_sum(ins[i : i + n_in], outs[o : o + n_out])
        else:
            terms(kind, orders, size, place_ref, hidden_ref, ins[i : i + n_in], outs[o : o + n_out])
        i, o = i + n_in, o + n_out


def step(size, place, hidden, token, jobs):
    ins = [x for _, _, given, _ in jobs for x in given]
    shapes = [s for _, _, _, made in jobs for s in made]
    counts = [(kind, orders, len(given), len(made)) for kind, orders, given, made in jobs]
    vmem, anywhere = pl.BlockSpec(memory_space=pltpu.VMEM), pl.BlockSpec(memory_space=pl.ANY)
    res = pl.pallas_call(
        functools.partial(step_kernel, size, counts),
        in_specs=[pl.BlockSpec(memory_space=pltpu.SMEM), vmem] + [vmem] * len(ins) + [anywhere],
        out_specs=[vmem] * len(shapes) + [anywhere],
        out_shape=shapes + [jax.ShapeDtypeStruct(token.shape, token.dtype)],
        input_output_aliases={2 + len(ins): len(shapes)},
        compiler_params=pltpu.CompilerParams(vmem_limit_bytes=VMEM),
    )(place, hidden, *ins, token)
    made, at = [], 0
    for _, _, _, n_out in counts:
        made.append(res[at : at + n_out])
        at += n_out
    return made, res[-1]


def shards(grad_out, route_probs, routes, hidden_saved):
    tok, model_cols = grad_out.shape
    flight, slot_count, hidden = hidden_saved.shape
    ranks = lax.axis_size("ep")
    peers = lax.axis_size("dp")
    capacity = slot_count // ranks
    size = hidden // peers
    dp = lax.axis_index("dp")
    place = jnp.stack([dp // 2, dp % 2]).astype(jnp.int32)
    token = jnp.zeros((8, 128), jnp.int32)
    vmem, anywhere = pl.BlockSpec(memory_space=pltpu.VMEM), pl.BlockSpec(memory_space=pl.ANY)
    partners = (
        [(i, i ^ 2) for i in range(peers)],
        [(i, (3 - i // 2) * 2 + i % 2) for i in range(peers)],
        [(i, i ^ 1) for i in range(peers)],
    )

    def shape(rows, cols, dtype=jnp.bfloat16):
        return jax.ShapeDtypeStruct((rows, cols), dtype)

    arrived, came, keep, out = {}, {}, {}, {}
    for names in STEPS:
        if names[0][0] == 0:
            c = names[0][1]
            width = sum(WIDTHS[c])
            start = sum(sum(w) for w in WIDTHS[:c])
            rows, token = pl.pallas_call(
                functools.partial(rows_kernel, ranks, capacity, start),
                in_specs=[vmem] * 3 + [anywhere],
                out_specs=[vmem, anywhere],
                out_shape=[shape(slot_count, width), jax.ShapeDtypeStruct(token.shape, token.dtype)],
                input_output_aliases={3: 1},
                compiler_params=pltpu.CompilerParams(vmem_limit_bytes=VMEM),
            )(routes.T, route_probs.T, grad_out, token)
            rows = rows.reshape(ranks, capacity, width)
            rows = lax.all_to_all(rows, "ep", split_axis=0, concat_axis=0, tiled=True)
            arrived[c], came[c] = rows.reshape(slot_count, width), []
            continue
        jobs = []
        for kind, c in names:
            if kind == 4:
                jobs.append((4, ORDERS[c], keep[c] + came[c][2 * len(ORDERS[c]) :], [shape(size, sum(WIDTHS[c]))]))
                continue
            made = [shape(hidden >> kind, w) for w in WIDTHS[c]]
            if kind == 3:
                made += [shape(size, w, jnp.float32) for w in WIDTHS[c]]
            jobs.append((kind, ORDERS[c], [arrived[c]] + came[c], made))
        results, token = step(size, place, hidden_saved[0], token, jobs)
        for (kind, c), made in zip(names, results):
            if kind == 4:
                out[c] = made[0]
                continue
            came[c] = came[c] + [
                lax.ppermute(m, "dp", partners[order[kind - 1]]) for m, order in zip(made, ORDERS[c])
            ]
            keep[c] = list(made[len(ORDERS[c]) :])
    return jnp.concatenate([out[c] for c in range(len(WIDTHS))], axis=1)


def solution(mesh):
    in_specs = (
        P(("ep", "dp"), None),
        P(("ep", "dp"), None),
        P(("ep", "dp"), None),
        P(("ep", "dp"), None, None),
    )
    return jax.shard_map(
        shards, mesh=mesh, in_specs=in_specs, out_specs=P("dp", "ep"), check_vma=False
    )
```

```python
import functools

import jax
import jax.numpy as jnp
from jax import lax
from jax.experimental import pallas as pl
from jax.experimental.pallas import tpu as pltpu
from jax.sharding import PartitionSpec as P

EXP_DEV = 4
TWO = ((0, 1, 2), (1, 0, 2))
THREE = ((0, 1, 2), (1, 2, 0), (2, 0, 1))
WIDTHS = ((384, 384), (768, 768), (512, 512, 256))
ORDERS = (TWO, TWO, THREE)
VMEM = 16 * 1024 * 1024
STEPS = (
    ((0, 0),),
    ((0, 1),),
    ((1, 0),),
    ((2, 0),),
    ((3, 0),),
    ((0, 2),),
    ((1, 1),),
    ((2, 1), (4, 0)),
    ((1, 2),),
    ((3, 1),),
    ((2, 2), (4, 1)),
    ((3, 2),),
    ((4, 2),),
)


def rows_kernel(columns, capacity, start, routes_ref, probs_ref, grad_ref, token_ref, out_ref, _):
    top, tok = routes_ref.shape
    ids = lax.broadcasted_iota(jnp.int32, (columns, tok), 0) * EXP_DEV
    named = jnp.zeros((columns, tok), jnp.float32)
    prob = jnp.zeros((columns, tok), jnp.float32)
    for k in range(top):
        hit = routes_ref[k : k + 1, :] == ids
        named = named + jnp.where(hit, 1.0, 0.0)
        prob = prob + jnp.where(hit, probs_ref[k : k + 1, :], 0.0)
    row = lax.broadcasted_iota(jnp.int32, (tok, tok), 0)
    col = lax.broadcasted_iota(jnp.int32, (tok, tok), 1)
    earlier = jnp.where(row < col, 1.0, 0.0).astype(jnp.bfloat16)
    slot = jnp.dot(named.astype(jnp.bfloat16), earlier, preferred_element_type=jnp.float32)
    slot = jnp.where(named > 0.0, slot, -1.0).astype(jnp.int32)
    places = lax.broadcasted_iota(jnp.int32, (columns, capacity, tok), 1)
    pick = slot[:, None, :] == places
    weight = jnp.sum(jnp.where(pick, prob[:, None, :], 0.0), axis=2, keepdims=True)
    weight = weight.reshape(columns * capacity, 1)
    pick = jnp.where(pick, 1.0, 0.0).reshape(columns * capacity, tok).astype(jnp.bfloat16)
    width = out_ref.shape[1]
    taken = jnp.dot(pick, grad_ref[:, start : start + width], preferred_element_type=jnp.float32)
    out_ref[...] = (weight * taken).astype(jnp.bfloat16)


def block_of(place_ref, order, bits):
    y, xh = place_ref[0], place_ref[1]
    for kind, bit in zip(order, bits):
        if bit:
            y, xh = (y ^ 1, xh) if kind == 0 else (3 - y, xh) if kind == 1 else (y, 1 - xh)
    return y * 2 + xh


def product(place_ref, hidden_ref, size, order, bits, rows):
    at = pl.multiple_of(block_of(place_ref, order, bits) * size, size)
    return lax.dot_general(
        hidden_ref[:, pl.ds(at, size)],
        rows,
        (((0,), (0,)), ((), ())),
        preferred_element_type=jnp.float32,
    )


def terms(kind, orders, size, place_ref, hidden_ref, ins, outs, sems):
    arrived_ref, came = ins[0], ins[1:]
    starts = [sum(out.shape[1] for out in outs[:part]) for part in range(len(orders))]
    spans = [pl.ds(start, out.shape[1]) for start, out in zip(starts, outs)]
    if kind == 1:
        held_ref = outs[-1]
        copies = [
            pltpu.make_async_copy(arrived_ref.at[:, span], held_ref.at[:, span], sems.at[part])
            for part, span in enumerate(spans)
        ]
        for copy in copies:
            copy.start()
        arrived_ref = held_ref
    for part, order in enumerate(orders):
        if kind == 1:
            copies[part].wait()
        rows = arrived_ref[:, spans[part]]
        earlier = [came[e * len(orders) + part] for e in range(kind - 1)]
        if kind == 1:
            targets = [(outs[part], (1, i, j)) for i in (1, 0) for j in (1, 0)]
        elif kind == 2:
            targets = [(outs[part], (0, 1, j)) for j in (1, 0)]
        else:
            targets = [(outs[part], (0, 0, 1)), (outs[len(orders) + part], (0, 0, 0))]
        filled = {}
        for out_ref, bits in targets:
            total = product(place_ref, hidden_ref, size, order, bits, rows)
            if kind > 1:
                at = (2 * (1 - bits[1]) + 1 - bits[2]) * size
                total = total + earlier[0][at : at + size, :].astype(jnp.float32)
            if kind > 2:
                at = (1 - bits[2]) * size
                total = total + earlier[1][at : at + size, :].astype(jnp.float32)
            at = filled.get(id(out_ref), 0)
            out_ref[at : at + size, :] = total.astype(out_ref.dtype)
            filled[id(out_ref)] = at + size


def last_sum(parts, ins, outs):
    start = 0
    for done in ins[2 * parts :]:
        width = done.shape[1]
        outs[0][:, start : start + width] = done[...]
        start += width
    for part in range(parts):
        width = ins[part].shape[1]
        total = ins[part][...] + ins[parts + part][...].astype(jnp.float32)
        outs[0][:, start : start + width] = total.astype(jnp.bfloat16)
        start += width


def step_kernel(size, jobs, place_ref, hidden_ref, *refs):
    ins = refs[: sum(n for _, _, n, _ in jobs)]
    outs = refs[len(ins) + 1 :]
    i = o = 0
    for kind, orders, n_in, n_out in jobs:
        if kind == 4:
            last_sum(len(orders), ins[i : i + n_in], outs[o : o + n_out])
        else:
            given, made = ins[i : i + n_in], outs[o : o + n_out]
            terms(kind, orders, size, place_ref, hidden_ref, given, made, refs[-1])
        i, o = i + n_in, o + n_out


def step(size, place, hidden, token, jobs):
    ins = [x for _, _, given, _ in jobs for x in given]
    shapes = [s for _, _, _, made in jobs for s in made]
    counts = [(kind, orders, len(given), len(made)) for kind, orders, given, made in jobs]
    vmem, anywhere = pl.BlockSpec(memory_space=pltpu.VMEM), pl.BlockSpec(memory_space=pl.ANY)
    res = pl.pallas_call(
        functools.partial(step_kernel, size, counts),
        in_specs=[pl.BlockSpec(memory_space=pltpu.SMEM), vmem]
        + [anywhere if kind == 1 else vmem for kind, _, given, _ in jobs for _ in given]
        + [anywhere],
        out_specs=[vmem] * len(shapes) + [anywhere],
        out_shape=shapes + [jax.ShapeDtypeStruct(token.shape, token.dtype)],
        input_output_aliases={2 + len(ins): len(shapes)},
        scratch_shapes=[pltpu.SemaphoreType.DMA((3,))],
        compiler_params=pltpu.CompilerParams(vmem_limit_bytes=VMEM),
    )(place, hidden, *ins, token)
    made, at = [], 0
    for _, _, _, n_out in counts:
        made.append(res[at : at + n_out])
        at += n_out
    return made, res[len(shapes)]


def shards(grad_out, route_probs, routes, hidden_saved):
    tok, model_cols = grad_out.shape
    flight, slot_count, hidden = hidden_saved.shape
    ranks = lax.axis_size("ep")
    peers = lax.axis_size("dp")
    capacity = slot_count // ranks
    size = hidden // peers
    dp = lax.axis_index("dp")
    place = jnp.stack([dp // 2, dp % 2]).astype(jnp.int32)
    token = jnp.zeros((8, 128), jnp.int32)
    vmem, anywhere = pl.BlockSpec(memory_space=pltpu.VMEM), pl.BlockSpec(memory_space=pl.ANY)
    partners = (
        [(i, i ^ 2) for i in range(peers)],
        [(i, (3 - i // 2) * 2 + i % 2) for i in range(peers)],
        [(i, i ^ 1) for i in range(peers)],
    )

    def shape(rows, cols, dtype=jnp.bfloat16):
        return jax.ShapeDtypeStruct((rows, cols), dtype)

    arrived, came, keep, out = {}, {}, {}, {}
    for names in STEPS:
        if names[0][0] == 0:
            c = names[0][1]
            width = sum(WIDTHS[c])
            start = sum(sum(w) for w in WIDTHS[:c])
            rows, token = pl.pallas_call(
                functools.partial(rows_kernel, ranks, capacity, start),
                in_specs=[vmem] * 3 + [anywhere],
                out_specs=[vmem, anywhere],
                out_shape=[shape(slot_count, width), jax.ShapeDtypeStruct(token.shape, token.dtype)],
                input_output_aliases={3: 1},
                compiler_params=pltpu.CompilerParams(vmem_limit_bytes=VMEM),
            )(routes.T, route_probs.T, grad_out, token)
            rows = rows.reshape(ranks, capacity, width)
            rows = lax.all_to_all(rows, "ep", split_axis=0, concat_axis=0, tiled=True)
            arrived[c], came[c] = rows.reshape(slot_count, width), []
            continue
        jobs = []
        for kind, c in names:
            if kind == 4:
                given, width = keep[c] + came[c][2 * len(ORDERS[c]) :], sum(WIDTHS[c])
                if c == len(WIDTHS) - 1:
                    given, width = given + [out[i] for i in range(c)], model_cols
                jobs.append((4, ORDERS[c], given, [shape(size, width)]))
                continue
            made = [shape(hidden >> kind, w) for w in WIDTHS[c]]
            if kind == 1:
                made.append(shape(slot_count, sum(WIDTHS[c])))
            if kind == 3:
                made += [shape(size, w, jnp.float32) for w in WIDTHS[c]]
            jobs.append((kind, ORDERS[c], [arrived[c]] + came[c], made))
        results, token = step(size, place, hidden_saved[0], token, jobs)
        for (kind, c), made in zip(names, results):
            if kind == 4:
                out[c] = made[0]
                continue
            came[c] = came[c] + [
                lax.ppermute(m, "dp", partners[order[kind - 1]]) for m, order in zip(made, ORDERS[c])
            ]
            if kind == 1:
                arrived[c] = made[-1]
            keep[c] = list(made[len(ORDERS[c]) :])
    return out[len(WIDTHS) - 1]


def solution(mesh):
    in_specs = (
        P(("ep", "dp"), None),
        P(("ep", "dp"), None),
        P(("ep", "dp"), None),
        P(("ep", "dp"), None, None),
    )
    return jax.shard_map(
        shards, mesh=mesh, in_specs=in_specs, out_specs=P("dp", "ep"), check_vma=False
    )
```

```python
import functools

import jax
import jax.numpy as jnp
from jax import lax
from jax.experimental import pallas as pl
from jax.experimental.pallas import tpu as pltpu
from jax.sharding import PartitionSpec as P

EXP_DEV = 4
TWO = ((0, 1, 2), (1, 0, 2))
THREE = ((0, 1, 2), (1, 2, 0), (2, 0, 1))
WIDTHS = ((384, 384), (768, 768), (512, 512, 256))
ORDERS = (TWO, TWO, THREE)
VMEM = 16 * 1024 * 1024
STEPS = (
    ((0, 0),),
    ((0, 1),),
    ((1, 0),),
    ((2, 0),),
    ((3, 0),),
    ((0, 2),),
    ((1, 1),),
    ((2, 1), (4, 0)),
    ((1, 2),),
    ((3, 1),),
    ((2, 2), (4, 1)),
    ((3, 2),),
    ((4, 2),),
)


def rows_kernel(columns, capacity, routes_ref, probs_ref, grad_ref, token_ref, out_ref, _):
    top, tok = routes_ref.shape
    ids = lax.broadcasted_iota(jnp.int32, (columns, tok), 0) * EXP_DEV
    named = jnp.zeros((columns, tok), jnp.float32)
    prob = jnp.zeros((columns, tok), jnp.float32)
    for k in range(top):
        hit = routes_ref[k : k + 1, :] == ids
        named = named + jnp.where(hit, 1.0, 0.0)
        prob = prob + jnp.where(hit, probs_ref[k : k + 1, :], 0.0)
    row = lax.broadcasted_iota(jnp.int32, (tok, tok), 0)
    col = lax.broadcasted_iota(jnp.int32, (tok, tok), 1)
    earlier = jnp.where(row < col, 1.0, 0.0).astype(jnp.bfloat16)
    slot = jnp.dot(named.astype(jnp.bfloat16), earlier, preferred_element_type=jnp.float32)
    slot = jnp.where(named > 0.0, slot, -1.0).astype(jnp.int32)
    places = lax.broadcasted_iota(jnp.int32, (columns, capacity, tok), 1)
    pick = slot[:, None, :] == places
    weight = jnp.sum(jnp.where(pick, prob[:, None, :], 0.0), axis=2, keepdims=True)
    weight = weight.reshape(columns * capacity, 1)
    pick = jnp.where(pick, 1.0, 0.0).reshape(columns * capacity, tok).astype(jnp.bfloat16)
    taken = jnp.dot(pick, grad_ref[...], preferred_element_type=jnp.float32)
    out_ref[...] = (weight * taken).astype(jnp.bfloat16)


def block_of(place_ref, order, bits):
    y, xh = place_ref[0], place_ref[1]
    for kind, bit in zip(order, bits):
        if bit:
            y, xh = (y ^ 1, xh) if kind == 0 else (3 - y, xh) if kind == 1 else (y, 1 - xh)
    return y * 2 + xh


def product(place_ref, hidden_ref, size, order, bits, rows):
    at = pl.multiple_of(block_of(place_ref, order, bits) * size, size)
    return lax.dot_general(
        hidden_ref[:, pl.ds(at, size)],
        rows,
        (((0,), (0,)), ((), ())),
        preferred_element_type=jnp.float32,
    )


def terms(kind, orders, size, place_ref, hidden_ref, ins, outs, sems):
    arrived_ref, came = ins[0], ins[1:]
    starts = [sum(out.shape[1] for out in outs[:part]) for part in range(len(orders))]
    spans = [pl.ds(start, out.shape[1]) for start, out in zip(starts, outs)]
    if kind == 1:
        held_ref = outs[-1]
        copies = [
            pltpu.make_async_copy(arrived_ref.at[:, span], held_ref.at[:, span], sems.at[part])
            for part, span in enumerate(spans)
        ]
        for copy in copies:
            copy.start()
        arrived_ref = held_ref
    for part, order in enumerate(orders):
        if kind == 1:
            copies[part].wait()
        rows = arrived_ref[:, spans[part]]
        earlier = [came[e * len(orders) + part] for e in range(kind - 1)]
        if kind == 1:
            targets = [(outs[part], (1, i, j)) for i in (1, 0) for j in (1, 0)]
        elif kind == 2:
            targets = [(outs[part], (0, 1, j)) for j in (1, 0)]
        else:
            targets = [(outs[part], (0, 0, 1)), (outs[len(orders) + part], (0, 0, 0))]
        filled = {}
        for out_ref, bits in targets:
            total = product(place_ref, hidden_ref, size, order, bits, rows)
            if kind > 1:
                at = (2 * (1 - bits[1]) + 1 - bits[2]) * size
                total = total + earlier[0][at : at + size, :].astype(jnp.float32)
            if kind > 2:
                at = (1 - bits[2]) * size
                total = total + earlier[1][at : at + size, :].astype(jnp.float32)
            at = filled.get(id(out_ref), 0)
            out_ref[at : at + size, :] = total.astype(out_ref.dtype)
            filled[id(out_ref)] = at + size


def last_sum(parts, ins, outs):
    start = 0
    for done in ins[2 * parts :]:
        width = done.shape[1]
        outs[0][:, start : start + width] = done[...]
        start += width
    for part in range(parts):
        width = ins[part].shape[1]
        total = ins[part][...] + ins[parts + part][...].astype(jnp.float32)
        outs[0][:, start : start + width] = total.astype(jnp.bfloat16)
        start += width


def step_kernel(size, jobs, place_ref, hidden_ref, *refs):
    ins = refs[: sum(n for _, _, n, _ in jobs)]
    outs = refs[len(ins) + 1 :]
    i = o = 0
    for kind, orders, n_in, n_out in jobs:
        if kind == 4:
            last_sum(len(orders), ins[i : i + n_in], outs[o : o + n_out])
        else:
            given, made = ins[i : i + n_in], outs[o : o + n_out]
            terms(kind, orders, size, place_ref, hidden_ref, given, made, refs[-1])
        i, o = i + n_in, o + n_out


def step(size, place, hidden, token, jobs):
    ins = [x for _, _, given, _ in jobs for x in given]
    shapes = [s for _, _, _, made in jobs for s in made]
    counts = [(kind, orders, len(given), len(made)) for kind, orders, given, made in jobs]
    vmem, anywhere = pl.BlockSpec(memory_space=pltpu.VMEM), pl.BlockSpec(memory_space=pl.ANY)
    res = pl.pallas_call(
        functools.partial(step_kernel, size, counts),
        in_specs=[pl.BlockSpec(memory_space=pltpu.SMEM), vmem]
        + [anywhere if kind == 1 else vmem for kind, _, given, _ in jobs for _ in given]
        + [anywhere],
        out_specs=[vmem] * len(shapes) + [anywhere],
        out_shape=shapes + [jax.ShapeDtypeStruct(token.shape, token.dtype)],
        input_output_aliases={2 + len(ins): len(shapes)},
        scratch_shapes=[pltpu.SemaphoreType.DMA((3,))],
        compiler_params=pltpu.CompilerParams(vmem_limit_bytes=VMEM),
    )(place, hidden, *ins, token)
    made, at = [], 0
    for _, _, _, n_out in counts:
        made.append(res[at : at + n_out])
        at += n_out
    return made, res[len(shapes)]


def shards(grad_out, route_probs, routes, hidden_saved):
    tok, model_cols = grad_out.shape
    flight, slot_count, hidden = hidden_saved.shape
    ranks = lax.axis_size("ep")
    peers = lax.axis_size("dp")
    capacity = slot_count // ranks
    size = hidden // peers
    dp = lax.axis_index("dp")
    place = jnp.stack([dp // 2, dp % 2]).astype(jnp.int32)
    token = jnp.zeros((8, 128), jnp.int32)
    vmem, anywhere = pl.BlockSpec(memory_space=pltpu.VMEM), pl.BlockSpec(memory_space=pl.ANY)
    partners = (
        [(i, i ^ 2) for i in range(peers)],
        [(i, (3 - i // 2) * 2 + i % 2) for i in range(peers)],
        [(i, i ^ 1) for i in range(peers)],
    )

    def shape(rows, cols, dtype=jnp.bfloat16):
        return jax.ShapeDtypeStruct((rows, cols), dtype)

    arrived, came, keep, out = {}, {}, {}, {}
    for names in STEPS:
        if names[0][0] == 0:
            c = names[0][1]
            width = sum(WIDTHS[c])
            start = sum(sum(w) for w in WIDTHS[:c])
            rows, token = pl.pallas_call(
                functools.partial(rows_kernel, ranks, capacity),
                in_specs=[vmem] * 3 + [anywhere],
                out_specs=[vmem, anywhere],
                out_shape=[shape(slot_count, width), jax.ShapeDtypeStruct(token.shape, token.dtype)],
                input_output_aliases={3: 1},
                compiler_params=pltpu.CompilerParams(vmem_limit_bytes=VMEM),
            )(routes.T, route_probs.T, grad_out[:, start : start + width], token)
            rows = rows.reshape(ranks, capacity, width)
            rows = lax.all_to_all(rows, "ep", split_axis=0, concat_axis=0, tiled=True)
            arrived[c], came[c] = rows.reshape(slot_count, width), []
            continue
        jobs = []
        for kind, c in names:
            if kind == 4:
                given, width = keep[c] + came[c][2 * len(ORDERS[c]) :], sum(WIDTHS[c])
                if c == len(WIDTHS) - 1:
                    given, width = given + [out[i] for i in range(c)], model_cols
                jobs.append((4, ORDERS[c], given, [shape(size, width)]))
                continue
            made = [shape(hidden >> kind, w) for w in WIDTHS[c]]
            if kind == 1:
                made.append(shape(slot_count, sum(WIDTHS[c])))
            if kind == 3:
                made += [shape(size, w, jnp.float32) for w in WIDTHS[c]]
            jobs.append((kind, ORDERS[c], [arrived[c]] + came[c], made))
        results, token = step(size, place, hidden_saved[0], token, jobs)
        for (kind, c), made in zip(names, results):
            if kind == 4:
                out[c] = made[0]
                continue
            came[c] = came[c] + [
                lax.ppermute(m, "dp", partners[order[kind - 1]]) for m, order in zip(made, ORDERS[c])
            ]
            if kind == 1:
                arrived[c] = made[-1]
            keep[c] = list(made[len(ORDERS[c]) :])
    return out[len(WIDTHS) - 1]


def solution(mesh):
    in_specs = (
        P(("ep", "dp"), None),
        P(("ep", "dp"), None),
        P(("ep", "dp"), None),
        P(("ep", "dp"), None, None),
    )
    return jax.shard_map(
        shards, mesh=mesh, in_specs=in_specs, out_specs=P("dp", "ep"), check_vma=False
    )
```
